128 devices in a mesh: head: 4 (over z), doc: 32 (over y, x, core).
Axes of the slice: x: 4, y: 4, z: 4, core: 2. Of those that a mesh axis runs over, the one named last changes fastest.
Arguments:
- packed_query_rows: bfloat16 [16384, 4096], P(('doc', 'head')), may hold values from -160 to 160
- packed_key_rows: bfloat16 [16384, 1024], P(('doc', 'head')), may hold values from -6 to 6
- packed_value_rows: bfloat16 [16384, 1024], P(('doc', 'head')), may hold values from -6 to 6
- doc_lengths: int32 [64], replicated, may hold values from 1 to 2048, 16384 in all
Outputs:
- attended: bfloat16 [16384, 4096], P(('doc', 'head'))
The draws below stay inside these ranges and needn't reach their ends.
Inputs may be any that keep to these rules, and one draw needn't show every extreme that they name: `doc_lengths`: the documents lie end to end in order and their lengths sum to 16384.
All inputs are finite; a program needn't handle non-finite values.
Results may differ from the reference program's by a relative error of at most 0.011.
Values may be sent and summed in bfloat16 or wider, within the bound.
A program may use at most 64 MiB of HBM per device.

```python
import math
import jax
import jax.numpy as jnp
import numpy as np
from jax import lax

QUERY_HEADS = 32
KEY_VALUE_HEADS = 8
HEAD_SIZE = 128
SEG = 512
SEQUENCE_TOKENS = 16384
DOCUMENT_LIMIT = 2048
DOCS = 64
N_DOC = 32


def drawn(key):
    document_sequences = jax.random.split(jax.random.fold_in(key, 7), 1)
    gathered_keys = jnp.clip(jax.random.normal(document_sequences[0], (SEQUENCE_TOKENS, KEY_VALUE_HEADS * HEAD_SIZE), jnp.float32), -6.0, 6.0)
    gathered_keys = gathered_keys.astype(jnp.bfloat16).astype(jnp.float32)
    return gathered_keys


def draw_packed_key_rows(key, part):
    gathered_keys = drawn(key)
    return gathered_keys.astype(jnp.bfloat16)


def draw_packed_query_rows(key, part):
    fresh_key = jax.random.fold_in(key, 13)
    query_tensor = jnp.clip(2.5 * jax.random.normal(fresh_key, (SEQUENCE_TOKENS, QUERY_HEADS * HEAD_SIZE), jnp.float32), -15.0, 15.0)
    return jnp.clip(query_tensor, -160.0, 160.0).astype(jnp.bfloat16)


def steps_of(rng, extent, cuts, least, high):
    level = 1.0
    for position, parts in cuts:
        heights = jax.random.uniform(jax.random.fold_in(jax.random.fold_in(rng, 6), position), (parts,), jnp.float32, least / len(cuts), high / len(cuts))
        level = level * jnp.repeat(jnp.exp(heights), extent[position] // parts).reshape((-1,) + (1,) * (len(extent) - 1 - position))
    return level


def length_profile(count, total, limit, skew):
    portions = [(1 << 20) // math.isqrt(grade ** skew) + 1 for grade in range(2, count + 1)]
    rest, counts = total - limit - (count - 1), [1] * (count - 1)
    while rest > 0:
        free = [i for i in range(count - 1) if counts[i] < limit]
        pool, left = sum([portions[i] for i in free]), rest
        for i in free:
            more = min(limit - counts[i], max(1, left * portions[i] // pool), rest)
            counts[i] = counts[i] + more
            rest = rest - more
    return np.array([limit] + counts)


def ragged(rng, amount, total, reach, lean):
    if amount == 2:
        one = jax.random.randint(rng, (), max(1, total - reach), min(reach, total - 1) + 1)
        return jnp.stack([one, total - one])
    tallies = jnp.asarray(length_profile(amount, total, reach, lean), jnp.int32)
    couples = (amount - 1) // 2
    donor, receiver = tallies[1:1 + 2 * couples:2], tallies[2:2 + 2 * couples:2]
    slack = jnp.minimum(donor - 1, reach - receiver)
    moved = jax.random.randint(jax.random.fold_in(rng, 1), (couples,), 0, 1 << 20) % (slack + 1)
    tallies = tallies.at[1:1 + 2 * couples:2].set(donor - moved).at[2:2 + 2 * couples:2].set(receiver + moved)
    return tallies[jax.random.permutation(jax.random.fold_in(rng, 2), amount)]


def noise(rng, dims, deviation, bound, shards=(), kind=jnp.bfloat16):
    entries = deviation * jax.random.normal(rng, dims, jnp.float32)
    if shards:
        entries = entries * steps_of(rng, dims, shards, -0.22, 0.18)
    return jnp.clip(entries, -bound, bound).astype(kind)


def setup_inputs(seed: int = 0) -> dict:
    key_of = jax.random.split(jax.random.key(seed), 5)
    return {
        "packed_query_rows": draw_packed_query_rows(jax.random.fold_in(key_of[4], 71), 0),
        "packed_key_rows": draw_packed_key_rows(jax.random.fold_in(key_of[4], 71), 0),
        "packed_value_rows": noise(key_of[2], (SEQUENCE_TOKENS, KEY_VALUE_HEADS * HEAD_SIZE), 1.0, 6.0, ((0, 128),)),
        "doc_lengths": ragged(key_of[3], DOCS, SEQUENCE_TOKENS, DOCUMENT_LIMIT, 2).astype(jnp.int32),
    }


NEGATIVE = -1e+30

def doc_starts(doc_lengths, positions):
    closing = jnp.cumsum(doc_lengths)
    passed = closing[None, :] <= positions[:, None]
    return lax.optimization_barrier(jnp.sum(jnp.where(passed, doc_lengths[None, :], 0), axis=1)).astype(jnp.int32)

def reference(packed_query_rows, packed_key_rows, packed_value_rows, doc_lengths):
    group_outputs = QUERY_HEADS // KEY_VALUE_HEADS
    factor = 1.0 / math.sqrt(HEAD_SIZE)
    query_tensor = packed_query_rows.reshape(SEQUENCE_TOKENS, KEY_VALUE_HEADS, group_outputs, HEAD_SIZE)
    filler_length = jnp.zeros((DOCUMENT_LIMIT, KEY_VALUE_HEADS * HEAD_SIZE), packed_key_rows.dtype)
    filled_key_rows = jnp.concatenate([filler_length, packed_key_rows], axis=0).reshape(DOCUMENT_LIMIT + SEQUENCE_TOKENS, KEY_VALUE_HEADS, HEAD_SIZE)
    filled_value_rows = jnp.concatenate([filler_length, packed_value_rows], axis=0).reshape(DOCUMENT_LIMIT + SEQUENCE_TOKENS, KEY_VALUE_HEADS, HEAD_SIZE)
    firsts = doc_starts(doc_lengths, jnp.arange(SEQUENCE_TOKENS, dtype=jnp.int32))

    def one_block(block_index):
        root = (block_index * SEG).astype(jnp.int32)
        block_queries = lax.dynamic_slice_in_dim(query_tensor, root, SEG, 0).astype(jnp.float32)
        block_keys = lax.dynamic_slice_in_dim(filled_key_rows, root, DOCUMENT_LIMIT + SEG, 0).astype(jnp.float32)
        block_values = lax.dynamic_slice_in_dim(filled_value_rows, root, DOCUMENT_LIMIT + SEG, 0).astype(jnp.float32)
        positions = root + jnp.arange(SEG, dtype=jnp.int32)
        key_positions = root - DOCUMENT_LIMIT + jnp.arange(DOCUMENT_LIMIT + SEG, dtype=jnp.int32)
        block_first = lax.dynamic_slice_in_dim(firsts, root, SEG, 0)
        visible = (key_positions[None, :] >= block_first[:, None]) & (key_positions[None, :] <= positions[:, None])

        def single_head(group_member):
            head_queries = lax.dynamic_index_in_dim(block_queries, group_member, 1, keepdims=False)
            head_keys = lax.dynamic_index_in_dim(block_keys, group_member, 1, keepdims=False)
            head_values = lax.dynamic_index_in_dim(block_values, group_member, 1, keepdims=False)
            scores = jnp.einsum('qgd,kd->gqk', head_queries, head_keys) * factor
            scores = jnp.where(visible[None], scores, NEGATIVE)
            highest = lax.optimization_barrier(jnp.max(scores, axis=2, keepdims=True))
            weights = jnp.where(visible[None], jnp.exp(scores - highest), 0.0)
            totals = lax.optimization_barrier(jnp.sum(weights, axis=2))
            rounded = lax.optimization_barrier(weights.astype(jnp.bfloat16)).astype(jnp.float32)
            summed = jnp.einsum('gqk,kd->qgd', rounded, head_values)
            return summed / totals.T[:, :, None]
        head_outputs = lax.map(single_head, jnp.arange(KEY_VALUE_HEADS, dtype=jnp.int32))
        return head_outputs.transpose(1, 0, 2, 3).reshape(SEG, QUERY_HEADS * HEAD_SIZE).astype(jnp.bfloat16)
    blocks = lax.map(one_block, jnp.arange(N_DOC, dtype=jnp.int32))
    return blocks.reshape(SEQUENCE_TOKENS, QUERY_HEADS * HEAD_SIZE)
```

```python
import functools
import math

import jax
import jax.numpy as jnp
from jax import lax
from jax.experimental import pallas as pl
from jax.experimental.pallas import tpu as pltpu
from jax.sharding import PartitionSpec as P

HEAD_SIZE = 128
GROUP = 4
TILE = 128
CHIP_TILES = 8
WINDOW_TILES = 24
REACH = 16
DOCS = 64
SCALE = math.log2(math.e) / math.sqrt(HEAD_SIZE)
HIDDEN = -1e30
MESH = pl.DeviceIdType.MESH
RELAY_FROM = 3
WIDE = 256


def kernel(
    lens_ref, q_ref, k_ref, v_ref, o_ref,
    qb, kvb, relay, feat_q, feat_k, s_scr, p_scr, ob,
    q_send, q_recv, k_send, k_recv, v_send, v_recv,
    x1_send, x1_recv, x2_send, x2_recv, relay_send, relay_recv, o_send, o_recv,
):
    z = lax.axis_index("head")
    d = lax.axis_index("doc")
    core = lax.rem(d, 2)
    c = lax.div(d, 2)
    x = lax.rem(c, 4)
    y = lax.div(c, 4)
    my_tile = core * 4 + z
    my_head = z * 2 + core

    def chip(yy, xx):
        return (lax.rem(yy + 4, 4) * 4 + lax.rem(xx + 4, 4)) * 2 + core

    ahead = lax.rem(d + 2, 32)
    behind = lax.rem(d + 30, 32)
    relay_to = chip(y, x - 1)
    relay_source = chip(y, x + 1)
    crossing = jnp.where((x == 1) | (x == 2), 1, 0)
    final_to = chip(y + crossing, x - 1)
    sender_crossing = jnp.where((x == 0) | (x == 1), 1, 0)
    final_from = chip(y - sender_crossing, x + 1)

    def column(g):
        return {"head": lax.div(g, 2), "doc": c * 2 + lax.rem(g, 2)}

    def along(dd):
        return {"head": z, "doc": dd}

    barrier = pltpu.get_barrier_semaphore()

    def greet(i, _):
        g = lax.rem(my_head + i, 8)
        pl.semaphore_signal(barrier, inc=1, device_id=column(g), device_id_type=MESH)
        return 0

    lax.fori_loop(1, 8, greet, 0)
    for other in (behind, relay_source, final_from):
        pl.semaphore_signal(barrier, inc=1, device_id=along(other), device_id_type=MESH)
    pl.semaphore_wait(barrier, 10)

    def rows(tile, count=1):
        return pl.ds(pl.multiple_of(tile * TILE, TILE), TILE * count)

    def cols(g, width):
        return pl.ds(pl.multiple_of(g * width, width), width)

    def k_copy(g, tile):
        return pltpu.make_async_remote_copy(
            src_ref=k_ref.at[:, cols(g, HEAD_SIZE)],
            dst_ref=kvb.at[0, rows(REACH + tile), :],
            send_sem=k_send.at[g], recv_sem=k_recv.at[tile],
            device_id=column(g), device_id_type=MESH)

    def v_copy(g, tile):
        return pltpu.make_async_remote_copy(
            src_ref=v_ref.at[:, cols(g, HEAD_SIZE)],
            dst_ref=kvb.at[1, rows(REACH + tile), :],
            send_sem=v_send.at[g], recv_sem=v_recv.at[tile],
            device_id=column(g), device_id_type=MESH)

    def q_copy(g, tile):
        return pltpu.make_async_remote_copy(
            src_ref=q_ref.at[:, cols(g, GROUP * HEAD_SIZE)],
            dst_ref=qb.at[tile],
            send_sem=q_send.at[g], recv_sem=q_recv.at[tile],
            device_id=column(g), device_id_type=MESH)

    def x1_copy(j):
        return pltpu.make_async_remote_copy(
            src_ref=kvb.at[:, rows(16 + j), :],
            dst_ref=kvb.at[:, rows(8 + j), :],
            send_sem=x1_send.at[j], recv_sem=x1_recv.at[j],
            device_id=along(ahead), device_id_type=MESH)

    def x2_copy(j):
        return pltpu.make_async_remote_copy(
            src_ref=kvb.at[:, rows(8 + j), :],
            dst_ref=kvb.at[:, rows(j), :],
            send_sem=x2_send.at[j], recv_sem=x2_recv.at[j],
            device_id=along(ahead), device_id_type=MESH)

    def relay_copy(j):
        return pltpu.make_async_remote_copy(
            src_ref=kvb.at[:, rows(16 + j), :],
            dst_ref=relay.at[j - RELAY_FROM],
            send_sem=relay_send.at[j], recv_sem=relay_recv.at[j],
            device_id=along(relay_to), device_id_type=MESH)

    def final_copy(j):
        return pltpu.make_async_remote_copy(
            src_ref=relay.at[j - RELAY_FROM],
            dst_ref=kvb.at[:, rows(j), :],
            send_sem=x2_send.at[j], recv_sem=x2_recv.at[j],
            device_id=along(final_to), device_id_type=MESH)

    def o_copy(g, tile):
        target = {"head": lax.rem(tile, 4), "doc": c * 2 + lax.div(tile, 4)}
        return pltpu.make_async_remote_copy(
            src_ref=ob.at[tile],
            dst_ref=o_ref.at[:, cols(g, GROUP * HEAD_SIZE)],
            send_sem=o_send.at[tile], recv_sem=o_recv.at[g],
            device_id=target, device_id_type=MESH)

    def send_kv(i, _):
        g = lax.rem(my_head + i, 8)
        k_copy(g, my_tile).start()
        v_copy(g, my_tile).start()
        return 0

    def send_q(i, _):
        g = lax.rem(my_head + i, 8)
        q_copy(g, my_tile).start()
        return 0

    lax.fori_loop(1, 8, send_kv, 0)
    pltpu.make_async_copy(
        k_ref.at[:, cols(my_head, HEAD_SIZE)], kvb.at[0, rows(REACH + my_tile), :], k_recv.at[my_tile]
    ).start()
    pltpu.make_async_copy(
        v_ref.at[:, cols(my_head, HEAD_SIZE)], kvb.at[1, rows(REACH + my_tile), :], v_recv.at[my_tile]
    ).start()
    lax.fori_loop(1, 8, send_q, 0)
    pltpu.make_async_copy(
        q_ref.at[:, cols(my_head, GROUP * HEAD_SIZE)], qb.at[my_tile], q_recv.at[my_tile]
    ).start()

    lane = lax.broadcasted_iota(jnp.int32, (1, 128), 1)

    def add_document(i, bounds):
        first, end = bounds
        length = lens_ref[i]
        return first + jnp.where(lane > i, length, 0), end + jnp.where(lane >= i, length, 0)

    zero = jnp.zeros((1, 128), jnp.int32)
    first, end = lax.fori_loop(0, DOCS, add_document, (zero, zero))
    first = jnp.where(lane == DOCS, -(1 << 30), first)
    end = jnp.where(lane == DOCS, 0, end)
    line = lax.broadcasted_iota(jnp.int32, (TILE, 128), 0)

    def member(tile):
        token = line + (c * CHIP_TILES - REACH + tile) * TILE
        return (token >= first) & (token < end)

    def key_features(tile, _):
        feat_k[rows(tile), :] = jnp.where(member(tile), 1.0, 0.0).astype(jnp.bfloat16)
        return 0

    def query_features(tile, _):
        feat_q[rows(tile), :] = jnp.where(member(tile + REACH), 0.0, HIDDEN).astype(jnp.bfloat16)
        return 0

    lax.fori_loop(0, WINDOW_TILES, key_features, 0)
    lax.fori_loop(0, CHIP_TILES, query_features, 0)

    def pass_own(t, _):
        j = CHIP_TILES - 1 - t
        k_copy(my_head, j).wait_recv()
        v_copy(my_head, j).wait_recv()
        x1_copy(j).start()

        @pl.when(j >= RELAY_FROM)
        def _():
            relay_copy(j).start()

        return 0

    lax.fori_loop(0, CHIP_TILES, pass_own, 0)

    def pass_on(t, _):
        j = CHIP_TILES - 1 - t
        x1_copy(j).wait_recv()

        @pl.when(j >= RELAY_FROM)
        def _():
            relay_copy(j).wait_recv()
            final_copy(j).start()

        @pl.when(j < RELAY_FROM)
        def _():
            x2_copy(j).start()

        return 0

    lax.fori_loop(0, CHIP_TILES, pass_on, 0)

    ones = jnp.ones(((REACH + 1) * TILE, 128), jnp.bfloat16)
    span = (REACH + 1) * TILE

    def attend(t, _):
        j = CHIP_TILES - 1 - t
        q_copy(my_head, j).wait_recv()
        x2_copy(j).wait_recv()
        queries = qb[j]
        features = feat_q[rows(j), :]
        left = jnp.concatenate(
            [queries[:, h * HEAD_SIZE:(h + 1) * HEAD_SIZE] for h in range(GROUP)], axis=0)
        left = jnp.concatenate([left, jnp.concatenate([features] * GROUP, axis=0)], axis=1)
        highest = None
        for at in range(0, span, WIDE):
            width = min(WIDE, span - at)
            part = pl.ds(pl.multiple_of(j * TILE + at, TILE), width)
            right = jnp.concatenate([kvb[0, part, :], feat_k[part, :]], axis=1)
            s = lax.dot_general(
                left, right, (((1,), (1,)), ((), ())), preferred_element_type=jnp.float32)
            if at + width == span:
                row = lax.rem(lax.broadcasted_iota(jnp.int32, s.shape, 0), TILE)
                col = lax.broadcasted_iota(jnp.int32, s.shape, 1) - (width - TILE)
                s = jnp.where(col <= row, s, HIDDEN)
            s_scr[:, at:at + width] = s
            for g in range(0, width, 128):
                piece = s[:, g:g + 128]
                highest = piece if highest is None else jnp.maximum(highest, piece)
        highest = jnp.max(highest, axis=1, keepdims=True)
        for at in range(0, span, WIDE):
            width = min(WIDE, span - at)
            p = jnp.exp2((s_scr[:, at:at + width] - highest) * SCALE)
            p_scr[:, at:at + width] = p.astype(jnp.bfloat16)
        values = jnp.concatenate([kvb[1, rows(j, REACH + 1), :], ones], axis=1)
        summed = jnp.dot(p_scr[...], values, preferred_element_type=jnp.float32)
        out = (summed[:, :HEAD_SIZE] / summed[:, HEAD_SIZE:]).astype(jnp.bfloat16)
        for h in range(GROUP):
            ob[j, :, h * HEAD_SIZE:(h + 1) * HEAD_SIZE] = out[h * TILE:(h + 1) * TILE]

        @pl.when(j != my_tile)
        def _():
            o_copy(my_head, j).start()

        @pl.when(j == my_tile)
        def _():
            pltpu.make_async_copy(
                ob.at[j], o_ref.at[:, cols(my_head, GROUP * HEAD_SIZE)], o_recv.at[my_head]
            ).start()

        return 0

    lax.fori_loop(0, CHIP_TILES, attend, 0)

    def finish(i, _):
        g = lax.rem(my_head + i, 8)
        o_copy(g, my_tile).wait_recv()
        x1_copy(i).wait_send()

        @pl.when(i >= RELAY_FROM)
        def _():
            relay_copy(i).wait_send()
            final_copy(i).wait_send()

        @pl.when(i < RELAY_FROM)
        def _():
            x2_copy(i).wait_send()

        @pl.when(i > 0)
        def _():
            k_copy(g, my_tile).wait_send()
            v_copy(g, my_tile).wait_send()
            q_copy(g, my_tile).wait_send()
            tile = lax.rem(my_tile + i, 8)
            o_copy(my_head, tile).wait_send()

        return 0

    lax.fori_loop(0, 8, finish, 0)


def on_device(packed_query_rows, packed_key_rows, packed_value_rows, doc_lengths):
    anywhere = pl.BlockSpec(memory_space=pl.ANY)
    bf16, f32 = jnp.bfloat16, jnp.float32
    dma = pltpu.SemaphoreType.DMA((8,))
    window = WINDOW_TILES * TILE
    span = (REACH + 1) * TILE
    return pl.pallas_call(
        kernel,
        out_shape=jax.ShapeDtypeStruct(packed_query_rows.shape, bf16),
        in_specs=[pl.BlockSpec(memory_space=pltpu.SMEM), anywhere, anywhere, anywhere],
        out_specs=anywhere,
        scratch_shapes=[
            pltpu.VMEM((CHIP_TILES, TILE, GROUP * HEAD_SIZE), bf16),
            pltpu.VMEM((2, window, HEAD_SIZE), bf16),
            pltpu.VMEM((CHIP_TILES - RELAY_FROM, 2, TILE, HEAD_SIZE), bf16),
            pltpu.VMEM((CHIP_TILES * TILE, 128), bf16),
            pltpu.VMEM((window, 128), bf16),
            pltpu.VMEM((GROUP * TILE, span), f32),
            pltpu.VMEM((GROUP * TILE, span), bf16),
            pltpu.VMEM((CHIP_TILES, TILE, GROUP * HEAD_SIZE), bf16),
        ] + [dma] * 14,
        compiler_params=pltpu.CompilerParams(
            collective_id=0, has_side_effects=True, vmem_limit_bytes=40 * 1024 * 1024),
        name="attention",
    )(doc_lengths, packed_query_rows, packed_key_rows, packed_value_rows)


def solution(mesh):
    token = P(("doc", "head"), None)
    return jax.shard_map(
        on_device, mesh=mesh, in_specs=(token, token, token, P()), out_specs=token, check_vma=False)
```

```python
import functools
import math

import jax
import jax.numpy as jnp
from jax import lax
from jax.experimental import pallas as pl
from jax.experimental.pallas import tpu as pltpu
from jax.sharding import PartitionSpec as P

HEAD_SIZE = 128
GROUP = 4
TILE = 128
CHIP_TILES = 8
WINDOW_TILES = 24
REACH = 16
DOCS = 64
SCALE = math.log2(math.e) / math.sqrt(HEAD_SIZE)
HIDDEN = -1e30
MESH = pl.DeviceIdType.MESH
RELAY_FROM = 3
SLAB = 256


def kernel(
    lens_ref, q_ref, k_ref, v_ref, o_ref,
    qb, kvb, relay, feat_q, feat_k, ob,
    q_send, q_recv, k_send, k_recv, v_send, v_recv,
    x1_send, x1_recv, x2_send, x2_recv, relay_send, relay_recv, o_send, o_recv,
):
    z = lax.axis_index("head")
    d = lax.axis_index("doc")
    core = lax.rem(d, 2)
    c = lax.div(d, 2)
    x = lax.rem(c, 4)
    y = lax.div(c, 4)
    my_tile = core * 4 + z
    my_head = z * 2 + core

    def chip(yy, xx):
        return (lax.rem(yy + 4, 4) * 4 + lax.rem(xx + 4, 4)) * 2 + core

    ahead = lax.rem(d + 2, 32)
    behind = lax.rem(d + 30, 32)
    relay_to = chip(y + jnp.where(x >= 2, 1, 0), x - 1)
    relay_source = chip(y - jnp.where((x == 1) | (x == 2), 1, 0), x + 1)
    final_to = chip(y, x - 1)
    final_from = chip(y, x + 1)

    def column(g):
        return {"head": lax.div(g, 2), "doc": c * 2 + lax.rem(g, 2)}

    def along(dd):
        return {"head": z, "doc": dd}

    barrier = pltpu.get_barrier_semaphore()

    def greet(i, _):
        g = lax.rem(my_head + i, 8)
        pl.semaphore_signal(barrier, inc=1, device_id=column(g), device_id_type=MESH)
        return 0

    lax.fori_loop(1, 8, greet, 0)
    for other in (behind, relay_source, final_from):
        pl.semaphore_signal(barrier, inc=1, device_id=along(other), device_id_type=MESH)
    pl.semaphore_wait(barrier, 10)

    def rows(tile, count=1):
        return pl.ds(pl.multiple_of(tile * TILE, TILE), TILE * count)

    def cols(g, width):
        return pl.ds(pl.multiple_of(g * width, width), width)

    def k_copy(g, tile):
        return pltpu.make_async_remote_copy(
            src_ref=k_ref.at[:, cols(g, HEAD_SIZE)],
            dst_ref=kvb.at[0, rows(REACH + tile), :],
            send_sem=k_send.at[g], recv_sem=k_recv.at[tile],
            device_id=column(g), device_id_type=MESH)

    def v_copy(g, tile):
        return pltpu.make_async_remote_copy(
            src_ref=v_ref.at[:, cols(g, HEAD_SIZE)],
            dst_ref=kvb.at[1, rows(REACH + tile), :],
            send_sem=v_send.at[g], recv_sem=v_recv.at[tile],
            device_id=column(g), device_id_type=MESH)

    def q_copy(g, tile):
        return pltpu.make_async_remote_copy(
            src_ref=q_ref.at[:, cols(g, GROUP * HEAD_SIZE)],
            dst_ref=qb.at[tile],
            send_sem=q_send.at[g], recv_sem=q_recv.at[tile],
            device_id=column(g), device_id_type=MESH)

    def x1_copy(j):
        return pltpu.make_async_remote_copy(
            src_ref=kvb.at[:, rows(16 + j), :],
            dst_ref=kvb.at[:, rows(8 + j), :],
            send_sem=x1_send.at[j], recv_sem=x1_recv.at[j],
            device_id=along(ahead), device_id_type=MESH)

    def x2_copy(j):
        return pltpu.make_async_remote_copy(
            src_ref=kvb.at[:, rows(8 + j), :],
            dst_ref=kvb.at[:, rows(j), :],
            send_sem=x2_send.at[j], recv_sem=x2_recv.at[j],
            device_id=along(ahead), device_id_type=MESH)

    def relay_copy(j):
        return pltpu.make_async_remote_copy(
            src_ref=kvb.at[:, rows(16 + j), :],
            dst_ref=relay.at[j - RELAY_FROM],
            send_sem=relay_send.at[j], recv_sem=relay_recv.at[j],
            device_id=along(relay_to), device_id_type=MESH)

    def final_copy(j):
        return pltpu.make_async_remote_copy(
            src_ref=relay.at[j - RELAY_FROM],
            dst_ref=kvb.at[:, rows(j), :],
            send_sem=x2_send.at[j], recv_sem=x2_recv.at[j],
            device_id=along(final_to), device_id_type=MESH)

    def o_copy(g, tile):
        target = {"head": lax.rem(tile, 4), "doc": c * 2 + lax.div(tile, 4)}
        return pltpu.make_async_remote_copy(
            src_ref=ob.at[tile],
            dst_ref=o_ref.at[:, cols(g, GROUP * HEAD_SIZE)],
            send_sem=o_send.at[tile], recv_sem=o_recv.at[g],
            device_id=target, device_id_type=MESH)

    def send_kv(i, _):
        g = lax.rem(my_head + i, 8)
        k_copy(g, my_tile).start()
        v_copy(g, my_tile).start()
        return 0

    def send_q(i, _):
        g = lax.rem(my_head + i, 8)
        q_copy(g, my_tile).start()
        return 0

    lax.fori_loop(1, 8, send_kv, 0)
    pltpu.make_async_copy(
        k_ref.at[:, cols(my_head, HEAD_SIZE)], kvb.at[0, rows(REACH + my_tile), :], k_recv.at[my_tile]
    ).start()
    pltpu.make_async_copy(
        v_ref.at[:, cols(my_head, HEAD_SIZE)], kvb.at[1, rows(REACH + my_tile), :], v_recv.at[my_tile]
    ).start()
    lax.fori_loop(1, 8, send_q, 0)
    pltpu.make_async_copy(
        q_ref.at[:, cols(my_head, GROUP * HEAD_SIZE)], qb.at[my_tile], q_recv.at[my_tile]
    ).start()

    lane = lax.broadcasted_iota(jnp.int32, (1, 128), 1)

    def add_document(i, bounds):
        first, end = bounds
        length = lens_ref[i]
        return first + jnp.where(lane > i, length, 0), end + jnp.where(lane >= i, length, 0)

    zero = jnp.zeros((1, 128), jnp.int32)
    first, end = lax.fori_loop(0, DOCS, add_document, (zero, zero))
    first = jnp.where(lane == DOCS, -(1 << 30), first)
    end = jnp.where(lane == DOCS, 0, end)
    line = lax.broadcasted_iota(jnp.int32, (TILE, 128), 0)

    def member(tile):
        token = line + (c * CHIP_TILES - REACH + tile) * TILE
        return (token >= first) & (token < end)

    def key_features(tile, _):
        feat_k[rows(tile), :] = jnp.where(member(tile), 1.0, 0.0).astype(jnp.bfloat16)
        return 0

    def query_features(tile, _):
        feat_q[rows(tile), :] = jnp.where(member(tile + REACH), 0.0, HIDDEN).astype(jnp.bfloat16)
        return 0

    lax.fori_loop(0, WINDOW_TILES, key_features, 0)
    lax.fori_loop(0, CHIP_TILES, query_features, 0)

    def pass_own(t, _):
        j = CHIP_TILES - 1 - t
        k_copy(my_head, j).wait_recv()
        v_copy(my_head, j).wait_recv()
        x1_copy(j).start()

        @pl.when(j >= RELAY_FROM)
        def _():
            relay_copy(j).start()

        return 0

    lax.fori_loop(0, CHIP_TILES, pass_own, 0)

    def pass_on(t, _):
        j = CHIP_TILES - 1 - t
        x1_copy(j).wait_recv()

        @pl.when(j >= RELAY_FROM)
        def _():
            relay_copy(j).wait_recv()
            final_copy(j).start()

        @pl.when(j < RELAY_FROM)
        def _():
            x2_copy(j).start()

        return 0

    lax.fori_loop(0, CHIP_TILES, pass_on, 0)

    ones = jnp.ones(((REACH + 1) * TILE, 128), jnp.bfloat16)
    span = (REACH + 1) * TILE
    causal = lax.broadcasted_iota(jnp.int32, (TILE, TILE), 1) <= lax.broadcasted_iota(
        jnp.int32, (TILE, TILE), 0)

    def attend(t, _):
        j = CHIP_TILES - 1 - t
        q_copy(my_head, j).wait_recv()
        x2_copy(j).wait_recv()
        queries = qb[j]
        features = feat_q[rows(j), :]
        left = jnp.concatenate(
            [queries[:, h * HEAD_SIZE:(h + 1) * HEAD_SIZE] for h in range(GROUP)], axis=0)
        left = jnp.concatenate([left, jnp.concatenate([features] * GROUP, axis=0)], axis=1)
        window = rows(j, REACH + 1)
        right = jnp.concatenate([kvb[0, window, :], feat_k[window, :]], axis=1)
        values = jnp.concatenate([kvb[1, window, :], ones], axis=1)
        slabs = [
            lax.dot_general(
                left[i:i + SLAB], right, (((1,), (1,)), ((), ())), preferred_element_type=jnp.float32)
            for i in range(0, GROUP * TILE, SLAB)]
        parts = []
        for i in range(0, GROUP * TILE, TILE):
            s = slabs[i // SLAB][i % SLAB:i % SLAB + TILE]
            s = jnp.concatenate(
                [s[:, :span - TILE], jnp.where(causal, s[:, span - TILE:], HIDDEN)], axis=1)
            highest = s[:, :128]
            for g in range(128, span, 128):
                highest = jnp.maximum(highest, s[:, g:g + 128])
            highest = jnp.max(highest, axis=1, keepdims=True)
            weights = jnp.exp2((s - highest) * SCALE).astype(jnp.bfloat16)
            parts.append(jnp.dot(weights, values, preferred_element_type=jnp.float32))
        summed = jnp.concatenate(parts, axis=0)
        out = (summed[:, :HEAD_SIZE] / summed[:, HEAD_SIZE:]).astype(jnp.bfloat16)
        for h in range(GROUP):
            ob[j, :, h * HEAD_SIZE:(h + 1) * HEAD_SIZE] = out[h * TILE:(h + 1) * TILE]

        @pl.when(j != my_tile)
        def _():
            o_copy(my_head, j).start()

        @pl.when(j == my_tile)
        def _():
            pltpu.make_async_copy(
                ob.at[j], o_ref.at[:, cols(my_head, GROUP * HEAD_SIZE)], o_recv.at[my_head]
            ).start()

        return 0

    lax.fori_loop(0, CHIP_TILES, attend, 0)

    def finish(i, _):
        g = lax.rem(my_head + i, 8)
        o_copy(g, my_tile).wait_recv()
        x1_copy(i).wait_send()

        @pl.when(i >= RELAY_FROM)
        def _():
            relay_copy(i).wait_send()
            final_copy(i).wait_send()

        @pl.when(i < RELAY_FROM)
        def _():
            x2_copy(i).wait_send()

        @pl.when(i > 0)
        def _():
            k_copy(g, my_tile).wait_send()
            v_copy(g, my_tile).wait_send()
            q_copy(g, my_tile).wait_send()
            tile = lax.rem(my_tile + i, 8)
            o_copy(my_head, tile).wait_send()

        return 0

    lax.fori_loop(0, 8, finish, 0)


def on_device(packed_query_rows, packed_key_rows, packed_value_rows, doc_lengths):
    anywhere = pl.BlockSpec(memory_space=pl.ANY)
    bf16, f32 = jnp.bfloat16, jnp.float32
    dma = pltpu.SemaphoreType.DMA((8,))
    window = WINDOW_TILES * TILE
    return pl.pallas_call(
        kernel,
        out_shape=jax.ShapeDtypeStruct(packed_query_rows.shape, bf16),
        in_specs=[pl.BlockSpec(memory_space=pltpu.SMEM), anywhere, anywhere, anywhere],
        out_specs=anywhere,
        scratch_shapes=[
            pltpu.VMEM((CHIP_TILES, TILE, GROUP * HEAD_SIZE), bf16),
            pltpu.VMEM((2, window, HEAD_SIZE), bf16),
            pltpu.VMEM((CHIP_TILES - RELAY_FROM, 2, TILE, HEAD_SIZE), bf16),
            pltpu.VMEM((CHIP_TILES * TILE, 128), bf16),
            pltpu.VMEM((window, 128), bf16),
            pltpu.VMEM((CHIP_TILES, TILE, GROUP * HEAD_SIZE), bf16),
        ] + [dma] * 14,
        compiler_params=pltpu.CompilerParams(
            collective_id=0, has_side_effects=True, vmem_limit_bytes=60 * 1024 * 1024),
        name="attention",
    )(doc_lengths, packed_query_rows, packed_key_rows, packed_value_rows)


def solution(mesh):
    token = P(("doc", "head"), None)
    return jax.shard_map(
        on_device, mesh=mesh, in_specs=(token, token, token, P()), out_specs=token, check_vma=False)
```

```python
import functools
import math

import jax
import jax.numpy as jnp
from jax import lax
from jax.experimental import pallas as pl
from jax.experimental.pallas import tpu as pltpu
from jax.sharding import PartitionSpec as P

HEAD_SIZE = 128
GROUP = 4
TILE = 128
CHIP_TILES = 8
WINDOW_TILES = 24
REACH = 16
DOCS = 64
SCALE = math.log2(math.e) / math.sqrt(HEAD_SIZE)
HIDDEN = -1e30
MESH = pl.DeviceIdType.MESH
RELAYED = 5
HALF = 2 * HEAD_SIZE
CHIPS = 16
NEAREST = ((0, 0), (0, 1), (1, 0), (3, 0), (1, 1), (3, 1), (2, 0), (2, 1))
SLAB = 256


def kernel(
    lens_ref, q_ref, k_ref, v_ref, o_ref,
    qb, kvb, relay, feat_q, feat_k, ob,
    q_send, q_recv, k_send, k_recv, v_send, v_recv,
    x1_send, x1_recv, x2_send, x2_recv, relay_send, relay_recv, final_send, o_send, o_recv,
):
    z = lax.axis_index("head")
    d = lax.axis_index("doc")
    core = lax.rem(d, 2)
    c = lax.div(d, 2)
    x = lax.rem(c, 4)
    y = lax.div(c, 4)
    my_tile = core * 4 + z
    my_head = z * 2 + core

    def chip(yy, xx):
        return (lax.rem(yy + 4, 4) * 4 + lax.rem(xx + 4, 4)) * 2 + core

    ahead = lax.rem(d + 2, 32)
    behind = lax.rem(d + 30, 32)
    relay_to = chip(y + jnp.where(x >= 2, 1, 0), x - 1)
    relay_source = chip(y - jnp.where((x == 1) | (x == 2), 1, 0), x + 1)
    final_to = chip(y, x - 1)
    final_from = chip(y, x + 1)

    def column(g):
        return {"head": lax.div(g, 2), "doc": c * 2 + lax.rem(g, 2)}

    def along(dd):
        return {"head": z, "doc": dd}

    barrier = pltpu.get_barrier_semaphore()

    def greet(i, _):
        g = lax.rem(my_head + i, 8)
        pl.semaphore_signal(barrier, inc=1, device_id=column(g), device_id_type=MESH)
        return 0

    lax.fori_loop(1, 8, greet, 0)
    for other in (behind, relay_source, final_from):
        pl.semaphore_signal(barrier, inc=1, device_id=along(other), device_id_type=MESH)
    pl.semaphore_wait(barrier, 10)

    def rows(tile, count=1):
        return pl.ds(pl.multiple_of(tile * TILE, TILE), TILE * count)

    def cols(g, width):
        return pl.ds(pl.multiple_of(g * width, width), width)

    def place(dz, dcore):
        zz, cc = lax.rem(z + dz, 4), lax.rem(core + dcore, 2)
        return zz * 2 + cc, cc * 4 + zz

    def k_copy(g, tile):
        return pltpu.make_async_remote_copy(
            src_ref=k_ref.at[:, cols(g, HEAD_SIZE)],
            dst_ref=kvb.at[0, rows(REACH + tile), :],
            send_sem=k_send.at[g], recv_sem=k_recv.at[tile],
            device_id=column(g), device_id_type=MESH)

    def v_copy(g, tile):
        return pltpu.make_async_remote_copy(
            src_ref=v_ref.at[:, cols(g, HEAD_SIZE)],
            dst_ref=kvb.at[1, rows(REACH + tile), :],
            send_sem=v_send.at[g], recv_sem=v_recv.at[tile],
            device_id=column(g), device_id_type=MESH)

    def q_copy(g, tile, half):
        return pltpu.make_async_remote_copy(
            src_ref=q_ref.at[:, cols(g * 2 + half, HALF)],
            dst_ref=qb.at[half, tile],
            send_sem=q_send.at[half, g], recv_sem=q_recv.at[half, tile],
            device_id=column(g), device_id_type=MESH)

    def x1_copy(j):
        return pltpu.make_async_remote_copy(
            src_ref=kvb.at[:, rows(16 + j), :],
            dst_ref=kvb.at[:, rows(8 + j), :],
            send_sem=x1_send.at[j], recv_sem=x1_recv.at[j],
            device_id=along(ahead), device_id_type=MESH)

    def x2_copy(j):
        return pltpu.make_async_remote_copy(
            src_ref=kvb.at[:, rows(8 + j), :],
            dst_ref=kvb.at[:, rows(j), :],
            send_sem=x2_send.at[j], recv_sem=x2_recv.at[j],
            device_id=along(ahead), device_id_type=MESH)

    def relay_copy(j, slot):
        return pltpu.make_async_remote_copy(
            src_ref=kvb.at[:, rows(16 + j), :],
            dst_ref=relay.at[slot],
            send_sem=relay_send.at[slot], recv_sem=relay_recv.at[slot],
            device_id=along(relay_to), device_id_type=MESH)

    def final_copy(j, slot):
        return pltpu.make_async_remote_copy(
            src_ref=relay.at[slot],
            dst_ref=kvb.at[:, rows(j), :],
            send_sem=final_send.at[slot], recv_sem=x2_recv.at[j],
            device_id=along(final_to), device_id_type=MESH)

    def o_copy(g, tile, half):
        target = {"head": lax.rem(tile, 4), "doc": c * 2 + lax.div(tile, 4)}
        return pltpu.make_async_remote_copy(
            src_ref=ob.at[half, tile],
            dst_ref=o_ref.at[:, cols(g * 2 + half, HALF)],
            send_sem=o_send.at[half, tile], recv_sem=o_recv.at[half, g],
            device_id=target, device_id_type=MESH)

    sends_one = c < CHIPS - 1
    sends_two = (c < CHIPS - 1) & (c > 0)
    starts_relay = c < CHIPS - 2
    is_relay = y * 4 + lax.rem(x + 3, 4) >= 2
    takes_one = c > 0
    takes_two = c > 1

    pltpu.make_async_copy(
        k_ref.at[:, cols(my_head, HEAD_SIZE)], kvb.at[0, rows(REACH + my_tile), :], k_recv.at[my_tile]
    ).start()
    pltpu.make_async_copy(
        v_ref.at[:, cols(my_head, HEAD_SIZE)], kvb.at[1, rows(REACH + my_tile), :], v_recv.at[my_tile]
    ).start()
    for at in NEAREST[1:]:
        g, _ = place(*at)
        k_copy(g, my_tile).start()
        v_copy(g, my_tile).start()
    for half in range(2):
        pltpu.make_async_copy(
            q_ref.at[:, cols(my_head * 2 + half, HALF)], qb.at[half, my_tile], q_recv.at[half, my_tile]
        ).start()
        for at in NEAREST[1:]:
            g, _ = place(*at)
            q_copy(g, my_tile, half).start()

    @pl.when(c == 0)
    def _():
        kvb[:, 0:REACH * TILE, :] = jnp.zeros((2, REACH * TILE, HEAD_SIZE), jnp.bfloat16)

    @pl.when(c == 1)
    def _():
        kvb[:, 0:CHIP_TILES * TILE, :] = jnp.zeros((2, CHIP_TILES * TILE, HEAD_SIZE), jnp.bfloat16)

    lane = lax.broadcasted_iota(jnp.int32, (1, 128), 1)

    def add_document(i, bounds):
        first, end = bounds
        length = lens_ref[i]
        return first + jnp.where(lane > i, length, 0), end + jnp.where(lane >= i, length, 0)

    zero = jnp.zeros((1, 128), jnp.int32)
    first, end = lax.fori_loop(0, DOCS, add_document, (zero, zero))
    first = jnp.where(lane == DOCS, -(1 << 30), first)
    end = jnp.where(lane == DOCS, 0, end)
    line = lax.broadcasted_iota(jnp.int32, (TILE, 128), 0)

    def member(tile):
        token = line + (c * CHIP_TILES - REACH + tile) * TILE
        return (token >= first) & (token < end)

    def key_features(tile, _):
        feat_k[rows(tile), :] = jnp.where(member(tile), 1.0, 0.0).astype(jnp.bfloat16)
        return 0

    def query_features(tile, _):
        feat_q[rows(tile), :] = jnp.where(member(tile + REACH), 0.0, HIDDEN).astype(jnp.bfloat16)
        return 0

    lax.fori_loop(0, WINDOW_TILES, key_features, 0)
    lax.fori_loop(0, CHIP_TILES, query_features, 0)

    for r, at in enumerate(NEAREST):
        _, j = place(*at)
        k_copy(my_head, j).wait_recv()
        v_copy(my_head, j).wait_recv()

        @pl.when(sends_one)
        def _():
            x1_copy(j).start()

        if r < RELAYED:
            @pl.when(starts_relay)
            def _():
                relay_copy(j, r).start()

    for r, at in enumerate(NEAREST):
        _, j = place(*at)

        if r < RELAYED:
            @pl.when(is_relay)
            def _():
                relay_copy(j, r).wait_recv()
                final_copy(j, r).start()

        @pl.when(takes_one)
        def _():
            x1_copy(j).wait_recv()

        if r >= RELAYED:
            @pl.when(sends_two)
            def _():
                x2_copy(j).start()

    ones = jnp.ones(((REACH + 1) * TILE, 128), jnp.bfloat16)
    span = (REACH + 1) * TILE
    causal = lax.broadcasted_iota(jnp.int32, (TILE, TILE), 1) <= lax.broadcasted_iota(
        jnp.int32, (TILE, TILE), 0)

    def attend(half, j):
        queries = qb[half, j]
        features = feat_q[rows(j), :]
        left = jnp.concatenate([queries[:, :HEAD_SIZE], queries[:, HEAD_SIZE:]], axis=0)
        left = jnp.concatenate([left, jnp.concatenate([features] * 2, axis=0)], axis=1)
        window = rows(j, REACH + 1)
        right = jnp.concatenate([kvb[0, window, :], feat_k[window, :]], axis=1)
        values = jnp.concatenate([kvb[1, window, :], ones], axis=1)
        slabs = [
            lax.dot_general(
                left[i:i + SLAB], right, (((1,), (1,)), ((), ())), preferred_element_type=jnp.float32)
            for i in range(0, 2 * TILE, SLAB)]
        parts = []
        for i in range(0, 2 * TILE, TILE):
            s = slabs[i // SLAB][i % SLAB:i % SLAB + TILE]
            s = jnp.concatenate(
                [s[:, :span - TILE], jnp.where(causal, s[:, span - TILE:], HIDDEN)], axis=1)
            highest = s[:, :128]
            for g in range(128, span, 128):
                highest = jnp.maximum(highest, s[:, g:g + 128])
            highest = jnp.max(highest, axis=1, keepdims=True)
            weights = jnp.exp2((s - highest) * SCALE).astype(jnp.bfloat16)
            parts.append(jnp.dot(weights, values, preferred_element_type=jnp.float32))
        summed = jnp.concatenate(parts, axis=0)
        out = (summed[:, :HEAD_SIZE] / summed[:, HEAD_SIZE:]).astype(jnp.bfloat16)
        for h in range(2):
            ob[half, j, :, h * HEAD_SIZE:(h + 1) * HEAD_SIZE] = out[h * TILE:(h + 1) * TILE]

        @pl.when(j != my_tile)
        def _():
            o_copy(my_head, j, half).start()

        @pl.when(j == my_tile)
        def _():
            pltpu.make_async_copy(
                ob.at[half, j], o_ref.at[:, cols(my_head * 2 + half, HALF)], o_recv.at[half, my_head]
            ).start()

    def first_half(t, _):
        j = CHIP_TILES - 1 - t
        q_copy(my_head, j, 0).wait_recv()

        @pl.when(takes_two)
        def _():
            x2_copy(j).wait_recv()

        attend(0, j)
        return 0

    def second_half(t, _):
        j = lax.rem(my_tile + 1 + t, CHIP_TILES)
        q_copy(my_head, j, 1).wait_recv()
        attend(1, j)
        return 0

    lax.fori_loop(0, CHIP_TILES, first_half, 0)
    lax.fori_loop(0, CHIP_TILES, second_half, 0)

    for r, at in enumerate(NEAREST):
        g, j = place(*at)

        @pl.when(sends_one)
        def _():
            x1_copy(j).wait_send()

        if r < RELAYED:
            @pl.when(starts_relay)
            def _():
                relay_copy(j, r).wait_send()

            @pl.when(is_relay)
            def _():
                final_copy(j, r).wait_send()
        else:
            @pl.when(sends_two)
            def _():
                x2_copy(j).wait_send()

        if r > 0:
            k_copy(g, my_tile).wait_send()
            v_copy(g, my_tile).wait_send()
        for half in range(2):
            if r > 0:
                q_copy(g, my_tile, half).wait_send()
                o_copy(my_head, j, half).wait_send()
            o_copy(g, my_tile, half).wait_recv()


def on_device(packed_query_rows, packed_key_rows, packed_value_rows, doc_lengths):
    anywhere = pl.BlockSpec(memory_space=pl.ANY)
    bf16, f32 = jnp.bfloat16, jnp.float32
    dma = pltpu.SemaphoreType.DMA((CHIP_TILES,))
    halves = pltpu.SemaphoreType.DMA((2, CHIP_TILES))
    window = WINDOW_TILES * TILE
    return pl.pallas_call(
        kernel,
        out_shape=jax.ShapeDtypeStruct(packed_query_rows.shape, bf16),
        in_specs=[pl.BlockSpec(memory_space=pltpu.SMEM), anywhere, anywhere, anywhere],
        out_specs=anywhere,
        scratch_shapes=[
            pltpu.VMEM((2, CHIP_TILES, TILE, HALF), bf16),
            pltpu.VMEM((2, window, HEAD_SIZE), bf16),
            pltpu.VMEM((RELAYED, 2, TILE, HEAD_SIZE), bf16),
            pltpu.VMEM((CHIP_TILES * TILE, 128), bf16),
            pltpu.VMEM((window, 128), bf16),
            pltpu.VMEM((2, CHIP_TILES, TILE, HALF), bf16),
        ] + [halves] * 2 + [dma] * 11 + [halves] * 2,
        compiler_params=pltpu.CompilerParams(
            collective_id=0, has_side_effects=True, vmem_limit_bytes=60 * 1024 * 1024),
        name="attention",
    )(doc_lengths, packed_query_rows, packed_key_rows, packed_value_rows)


def solution(mesh):
    token = P(("doc", "head"), None)
    return jax.shard_map(
        on_device, mesh=mesh, in_specs=(token, token, token, P()), out_specs=token, check_vma=False)
```

```python
import functools
import math

import jax
import jax.numpy as jnp
from jax import lax
from jax.experimental import pallas as pl
from jax.experimental.pallas import tpu as pltpu
from jax.sharding import PartitionSpec as P

HEAD_SIZE = 128
TILE = 128
CHIP_TILES = 8
WINDOW_TILES = 24
REACH = 16
DOCS = 64
SCALE = math.log2(math.e) / math.sqrt(HEAD_SIZE)
HIDDEN = -1e30
MESH = pl.DeviceIdType.MESH
RELAYED = (7, 6, 5, 3, 1)
HALF = 2 * HEAD_SIZE
CHIPS = 16
NEAREST = ((0, 0), (0, 1), (1, 0), (3, 0), (1, 1), (3, 1), (2, 0), (2, 1))


def kernel(
    lens_ref, q_ref, k_ref, v_ref, o_ref,
    qb, kvb, kt, relay, feat_q, ob,
    q_send, q_recv, k_send, k_recv, v_send, v_recv,
    x1_send, x1_recv, x2_send, x2_recv, relay_send, relay_recv, final_send, o_send, o_recv,
):
    z = lax.axis_index("head")
    d = lax.axis_index("doc")
    core = lax.rem(d, 2)
    c = lax.div(d, 2)
    x = lax.rem(c, 4)
    y = lax.div(c, 4)
    my_tile = core * 4 + z
    my_head = z * 2 + core

    def chip(yy, xx):
        return (lax.rem(yy + 4, 4) * 4 + lax.rem(xx + 4, 4)) * 2 + core

    ahead = lax.rem(d + 2, 32)
    behind = lax.rem(d + 30, 32)
    relay_to = chip(y + jnp.where(x >= 2, 1, 0), x - 1)
    relay_source = chip(y - jnp.where((x == 1) | (x == 2), 1, 0), x + 1)
    final_to = chip(y, x - 1)
    final_from = chip(y, x + 1)

    def column(g):
        return {"head": lax.div(g, 2), "doc": c * 2 + lax.rem(g, 2)}

    def along(dd):
        return {"head": z, "doc": dd}

    barrier = pltpu.get_barrier_semaphore()

    def greet(i, _):
        g = lax.rem(my_head + i, 8)
        pl.semaphore_signal(barrier, inc=1, device_id=column(g), device_id_type=MESH)
        return 0

    lax.fori_loop(1, 8, greet, 0)
    for other in (behind, relay_source, final_from):
        pl.semaphore_signal(barrier, inc=1, device_id=along(other), device_id_type=MESH)
    pl.semaphore_wait(barrier, 10)

    def rows(tile, count=1):
        return pl.ds(pl.multiple_of(tile * TILE, TILE), TILE * count)

    def cols(g, width):
        return pl.ds(pl.multiple_of(g * width, width), width)

    def place(dz, dcore):
        zz, cc = lax.rem(z + dz, 4), lax.rem(core + dcore, 2)
        return zz * 2 + cc, cc * 4 + zz

    def k_copy(g, tile):
        return pltpu.make_async_remote_copy(
            src_ref=k_ref.at[:, cols(g, HEAD_SIZE)],
            dst_ref=kvb.at[0, rows(REACH + tile), :],
            send_sem=k_send.at[g], recv_sem=k_recv.at[tile],
            device_id=column(g), device_id_type=MESH)

    def v_copy(g, tile):
        return pltpu.make_async_remote_copy(
            src_ref=v_ref.at[:, cols(g, HEAD_SIZE)],
            dst_ref=kvb.at[1, rows(REACH + tile), :],
            send_sem=v_send.at[g], recv_sem=v_recv.at[tile],
            device_id=column(g), device_id_type=MESH)

    def q_copy(g, tile, half):
        return pltpu.make_async_remote_copy(
            src_ref=q_ref.at[:, cols(g * 2 + half, HALF)],
            dst_ref=qb.at[half, tile],
            send_sem=q_send.at[half, g], recv_sem=q_recv.at[half, tile],
            device_id=column(g), device_id_type=MESH)

    def x1_copy(j):
        return pltpu.make_async_remote_copy(
            src_ref=kvb.at[:, rows(16 + j), :],
            dst_ref=kvb.at[:, rows(8 + j), :],
            send_sem=x1_send.at[j], recv_sem=x1_recv.at[j],
            device_id=along(ahead), device_id_type=MESH)

    def x2_copy(j):
        return pltpu.make_async_remote_copy(
            src_ref=kvb.at[:, rows(8 + j), :],
            dst_ref=kvb.at[:, rows(j), :],
            send_sem=x2_send.at[j], recv_sem=x2_recv.at[j],
            device_id=along(ahead), device_id_type=MESH)

    def goes_round(j):
        return (lax.rem(j, 2) == 1) | (j == 6)

    def relay_copy(j):
        return pltpu.make_async_remote_copy(
            src_ref=kvb.at[:, rows(16 + j), :],
            dst_ref=relay.at[j],
            send_sem=relay_send.at[j], recv_sem=relay_recv.at[j],
            device_id=along(relay_to), device_id_type=MESH)

    def final_copy(j):
        return pltpu.make_async_remote_copy(
            src_ref=relay.at[j],
            dst_ref=kvb.at[:, rows(j), :],
            send_sem=final_send.at[j], recv_sem=x2_recv.at[j],
            device_id=along(final_to), device_id_type=MESH)

    def o_copy(g, tile, half):
        target = {"head": lax.rem(tile, 4), "doc": c * 2 + lax.div(tile, 4)}
        return pltpu.make_async_remote_copy(
            src_ref=ob.at[half, tile],
            dst_ref=o_ref.at[:, cols(g * 2 + half, HALF)],
            send_sem=o_send.at[half, tile], recv_sem=o_recv.at[half, g],
            device_id=target, device_id_type=MESH)

    sends_one = c < CHIPS - 1
    sends_two = (c < CHIPS - 1) & (c > 0)
    starts_relay = c < CHIPS - 2
    is_relay = y * 4 + lax.rem(x + 3, 4) >= 2
    takes_one = c > 0
    takes_two = c > 1

    pltpu.make_async_copy(
        k_ref.at[:, cols(my_head, HEAD_SIZE)], kvb.at[0, rows(REACH + my_tile), :], k_recv.at[my_tile]
    ).start()
    pltpu.make_async_copy(
        v_ref.at[:, cols(my_head, HEAD_SIZE)], kvb.at[1, rows(REACH + my_tile), :], v_recv.at[my_tile]
    ).start()
    for at in NEAREST[1:]:
        g, _ = place(*at)
        k_copy(g, my_tile).start()
        v_copy(g, my_tile).start()
    for half in range(2):
        pltpu.make_async_copy(
            q_ref.at[:, cols(my_head * 2 + half, HALF)], qb.at[half, my_tile], q_recv.at[half, my_tile]
        ).start()
        for at in NEAREST[1:]:
            g, _ = place(*at)
            q_copy(g, my_tile, half).start()

    @pl.when(c == 0)
    def _():
        kvb[:, 0:REACH * TILE, :] = jnp.zeros((2, REACH * TILE, HEAD_SIZE), jnp.bfloat16)

    @pl.when(c == 1)
    def _():
        kvb[:, 0:CHIP_TILES * TILE, :] = jnp.zeros((2, CHIP_TILES * TILE, HEAD_SIZE), jnp.bfloat16)

    lane = lax.broadcasted_iota(jnp.int32, (1, 128), 1)

    def add_document(i, bounds):
        first, end = bounds
        length = lens_ref[i]
        return first + jnp.where(lane > i, length, 0), end + jnp.where(lane >= i, length, 0)

    zero = jnp.zeros((1, 128), jnp.int32)
    first, end = lax.fori_loop(0, DOCS, add_document, (zero, zero))
    first = jnp.where(lane == DOCS, -(1 << 30), first)
    end = jnp.where(lane == DOCS, 0, end)
    line = lax.broadcasted_iota(jnp.int32, (TILE, 128), 0)

    def member(tile):
        token = line + (c * CHIP_TILES - REACH + tile) * TILE
        return (token >= first) & (token < end)

    def key_features(tile, _):
        kt[HEAD_SIZE:, rows(tile)] = jnp.where(member(tile), 1.0, 0.0).astype(jnp.bfloat16).T
        return 0

    def query_features(tile, _):
        feat_q[rows(tile), :] = jnp.where(member(tile + REACH), 0.0, HIDDEN).astype(jnp.bfloat16)
        return 0

    lax.fori_loop(0, WINDOW_TILES, key_features, 0)
    lax.fori_loop(0, CHIP_TILES, query_features, 0)

    def turn(tile):
        kt[:HEAD_SIZE, rows(tile)] = kvb[0, rows(tile), :].T

    for r, at in enumerate(NEAREST):
        _, j = place(*at)
        k_copy(my_head, j).wait_recv()
        v_copy(my_head, j).wait_recv()

        @pl.when(sends_one)
        def _():
            x1_copy(j).start()

        @pl.when(starts_relay & goes_round(j))
        def _():
            relay_copy(j).start()

        turn(REACH + j)

    for r, at in enumerate(NEAREST):
        _, j = place(*at)

        @pl.when(takes_one)
        def _():
            x1_copy(j).wait_recv()

        @pl.when(sends_two & jnp.logical_not(goes_round(j)))
        def _():
            x2_copy(j).start()

        if r >= CHIP_TILES - len(RELAYED):
            @pl.when(is_relay)
            def _():
                relayed = RELAYED[r - CHIP_TILES + len(RELAYED)]
                relay_copy(relayed).wait_recv()
                final_copy(relayed).start()

        turn(CHIP_TILES + j)

    ones = jnp.ones(((REACH + 1) * TILE, 128), jnp.bfloat16)
    span = (REACH + 1) * TILE
    causal = lax.broadcasted_iota(jnp.int32, (TILE, TILE), 1) <= lax.broadcasted_iota(
        jnp.int32, (TILE, TILE), 0)

    def scores(half, j, h):
        queries = qb[half, j, :, h * HEAD_SIZE:(h + 1) * HEAD_SIZE]
        left = jnp.concatenate([queries, feat_q[rows(j), :]], axis=1)
        s = jnp.dot(left, kt[:, rows(j, REACH + 1)], preferred_element_type=jnp.float32)
        return jnp.concatenate(
            [s[:, :span - TILE], jnp.where(causal, s[:, span - TILE:], HIDDEN)], axis=1)

    def weigh(half, j, h, s):
        highest = s[:, :128]
        for g in range(128, span, 128):
            highest = jnp.maximum(highest, s[:, g:g + 128])
        highest = jnp.max(highest, axis=1, keepdims=True)
        weights = jnp.exp2((s - highest) * SCALE).astype(jnp.bfloat16)
        values = jnp.concatenate([kvb[1, rows(j, REACH + 1), :], ones], axis=1)
        summed = jnp.dot(weights, values, preferred_element_type=jnp.float32)
        out = summed[:, :HEAD_SIZE] / summed[:, HEAD_SIZE:]
        ob[half, j, :, h * HEAD_SIZE:(h + 1) * HEAD_SIZE] = out.astype(jnp.bfloat16)

    def attend(half, tiles):
        units = [(j, h) for j in tiles for h in range(2)]
        scored = [scores(half, j, h) for j, h in units]
        for (j, h), s in zip(units, scored):
            weigh(half, j, h, s)
        for j in tiles:
            @pl.when(j != my_tile)
            def _():
                o_copy(my_head, j, half).start()

            @pl.when(j == my_tile)
            def _():
                pltpu.make_async_copy(
                    ob.at[half, j], o_ref.at[:, cols(my_head * 2 + half, HALF)],
                    o_recv.at[half, my_head]
                ).start()

    def first_half(t, _):
        tiles = (CHIP_TILES - 1 - 2 * t, CHIP_TILES - 2 - 2 * t)
        for j in tiles:
            q_copy(my_head, j, 0).wait_recv()

            @pl.when(takes_two)
            def _():
                x2_copy(j).wait_recv()

            turn(j)
        attend(0, tiles)
        return 0

    def second_half(t, _):
        tiles = tuple(lax.rem(my_tile + 2 * t + n, CHIP_TILES) for n in (1, 2))
        for j in tiles:
            q_copy(my_head, j, 1).wait_recv()
        attend(1, tiles)
        return 0

    lax.fori_loop(0, CHIP_TILES // 2, first_half, 0)
    lax.fori_loop(0, CHIP_TILES // 2, second_half, 0)
    for r, at in enumerate(NEAREST):
        g, j = place(*at)

        @pl.when(sends_one)
        def _():
            x1_copy(j).wait_send()

        @pl.when(starts_relay & goes_round(j))
        def _():
            relay_copy(j).wait_send()

        @pl.when(sends_two & jnp.logical_not(goes_round(j)))
        def _():
            x2_copy(j).wait_send()

        if r < len(RELAYED):
            @pl.when(is_relay)
            def _():
                final_copy(RELAYED[r]).wait_send()

        if r > 0:
            k_copy(g, my_tile).wait_send()
            v_copy(g, my_tile).wait_send()
        for half in range(2):
            if r > 0:
                q_copy(g, my_tile, half).wait_send()
                o_copy(my_head, j, half).wait_send()
            o_copy(g, my_tile, half).wait_recv()


def on_device(packed_query_rows, packed_key_rows, packed_value_rows, doc_lengths):
    anywhere = pl.BlockSpec(memory_space=pl.ANY)
    bf16, f32 = jnp.bfloat16, jnp.float32
    dma = pltpu.SemaphoreType.DMA((CHIP_TILES,))
    halves = pltpu.SemaphoreType.DMA((2, CHIP_TILES))
    window = WINDOW_TILES * TILE
    return pl.pallas_call(
        kernel,
        out_shape=jax.ShapeDtypeStruct(packed_query_rows.shape, bf16),
        in_specs=[pl.BlockSpec(memory_space=pltpu.SMEM), anywhere, anywhere, anywhere],
        out_specs=anywhere,
        scratch_shapes=[
            pltpu.VMEM((2, CHIP_TILES, TILE, HALF), bf16),
            pltpu.VMEM((2, window, HEAD_SIZE), bf16),
            pltpu.VMEM((2 * HEAD_SIZE, window), bf16),
            pltpu.VMEM((CHIP_TILES, 2, TILE, HEAD_SIZE), bf16),
            pltpu.VMEM((CHIP_TILES * TILE, 128), bf16),
            pltpu.VMEM((2, CHIP_TILES, TILE, HALF), bf16),
        ] + [halves] * 2 + [dma] * 11 + [halves] * 2,
        compiler_params=pltpu.CompilerParams(
            collective_id=0, has_side_effects=True, vmem_limit_bytes=60 * 1024 * 1024),
        name="attention",
    )(doc_lengths, packed_query_rows, packed_key_rows, packed_value_rows)


def solution(mesh):
    token = P(("doc", "head"), None)
    return jax.shard_map(
        on_device, mesh=mesh, in_specs=(token, token, token, P()), out_specs=token, check_vma=False)
```

```python
import functools
import math

import jax
import jax.numpy as jnp
from jax import lax
from jax.experimental import pallas as pl
from jax.experimental.pallas import tpu as pltpu
from jax.sharding import PartitionSpec as P

HEAD_SIZE = 128
TILE = 128
CHIP_TILES = 8
WINDOW_TILES = 24
REACH = 16
DOCS = 64
SCALE = math.log2(math.e) / math.sqrt(HEAD_SIZE)
HIDDEN = -1e30
MESH = pl.DeviceIdType.MESH
RELAYED = (7, 6, 5, 3, 1)
HALF = 2 * HEAD_SIZE
CHIPS = 16
FROM_FIRST = ((0, 1), (1, 1), (3, 1), (2, 1), (1, 0), (3, 0), (2, 0))
FROM_SECOND = ((1, 1), (3, 1), (2, 1), (0, 0), (1, 0), (3, 0), (2, 0))
HELD = 0
NEAREST = ((0, 0), (0, 1), (1, 0), (3, 0), (1, 1), (3, 1), (2, 0), (2, 1))


def kernel(
    lens_ref, q_ref, k_ref, v_ref, o_ref,
    qb, kvb, kt, relay, feat_q, ob,
    q_send, q_recv, k_send, k_recv, v_send, v_recv,
    x1_send, x1_recv, x2_send, x2_recv, relay_send, relay_recv, final_send, o_send, o_recv,
):
    z = lax.axis_index("head")
    d = lax.axis_index("doc")
    core = lax.rem(d, 2)
    c = lax.div(d, 2)
    x = lax.rem(c, 4)
    y = lax.div(c, 4)
    my_tile = core * 4 + z
    my_head = z * 2 + core

    def chip(yy, xx):
        return (lax.rem(yy + 4, 4) * 4 + lax.rem(xx + 4, 4)) * 2 + core

    ahead = lax.rem(d + 2, 32)
    behind = lax.rem(d + 30, 32)
    relay_to = chip(y + jnp.where(x >= 2, 1, 0), x - 1)
    relay_source = chip(y - jnp.where((x == 1) | (x == 2), 1, 0), x + 1)
    final_to = chip(y, x - 1)
    final_from = chip(y, x + 1)

    def column(g):
        return {"head": lax.div(g, 2), "doc": c * 2 + lax.rem(g, 2)}

    def along(dd):
        return {"head": z, "doc": dd}

    def rows(tile, count=1):
        return pl.ds(pl.multiple_of(tile * TILE, TILE), TILE * count)

    def cols(g, width):
        return pl.ds(pl.multiple_of(g * width, width), width)

    pltpu.make_async_copy(
        k_ref.at[:, cols(my_head, HEAD_SIZE)], kvb.at[0, rows(REACH + my_tile), :], k_recv.at[my_tile]
    ).start()
    pltpu.make_async_copy(
        v_ref.at[:, cols(my_head, HEAD_SIZE)], kvb.at[1, rows(REACH + my_tile), :], v_recv.at[my_tile]
    ).start()
    barrier = pltpu.get_barrier_semaphore()

    def greet(i, _):
        g = lax.rem(my_head + i, 8)
        pl.semaphore_signal(barrier, inc=1, device_id=column(g), device_id_type=MESH)
        return 0

    lax.fori_loop(1, 8, greet, 0)
    for other in (behind, relay_source, final_from):
        pl.semaphore_signal(barrier, inc=1, device_id=along(other), device_id_type=MESH)
    @pl.when(c == 0)
    def _():
        kvb[:, 0:REACH * TILE, :] = jnp.zeros((2, REACH * TILE, HEAD_SIZE), jnp.bfloat16)

    @pl.when(c == 1)
    def _():
        kvb[:, 0:CHIP_TILES * TILE, :] = jnp.zeros((2, CHIP_TILES * TILE, HEAD_SIZE), jnp.bfloat16)

    lane = lax.broadcasted_iota(jnp.int32, (1, 128), 1)

    def add_document(i, bounds):
        first, end = bounds
        length = lens_ref[i]
        return first + jnp.where(lane > i, length, 0), end + jnp.where(lane >= i, length, 0)

    zero = jnp.zeros((1, 128), jnp.int32)
    first, end = lax.fori_loop(0, DOCS, add_document, (zero, zero))
    first = jnp.where(lane == DOCS, -(1 << 30), first)
    end = jnp.where(lane == DOCS, 0, end)
    line = lax.broadcasted_iota(jnp.int32, (TILE, 128), 0)

    def member(tile):
        token = line + (c * CHIP_TILES - REACH + tile) * TILE
        return (token >= first) & (token < end)

    def key_features(tile, _):
        kt[HEAD_SIZE:, rows(tile)] = jnp.where(member(tile), 1.0, 0.0).astype(jnp.bfloat16).T
        return 0

    def query_features(tile, _):
        feat_q[rows(tile), :] = jnp.where(member(tile + REACH), 0.0, HIDDEN).astype(jnp.bfloat16)
        return 0

    lax.fori_loop(0, WINDOW_TILES, key_features, 0)
    lax.fori_loop(0, CHIP_TILES, query_features, 0)

    pl.semaphore_wait(barrier, 10)


    def place(dz, dcore):
        zz, cc = lax.rem(z + dz, 4), lax.rem(core + dcore, 2)
        return zz * 2 + cc, cc * 4 + zz

    def k_copy(g, tile):
        return pltpu.make_async_remote_copy(
            src_ref=k_ref.at[:, cols(g, HEAD_SIZE)],
            dst_ref=kvb.at[0, rows(REACH + tile), :],
            send_sem=k_send.at[g], recv_sem=k_recv.at[tile],
            device_id=column(g), device_id_type=MESH)

    def v_copy(g, tile):
        return pltpu.make_async_remote_copy(
            src_ref=v_ref.at[:, cols(g, HEAD_SIZE)],
            dst_ref=kvb.at[1, rows(REACH + tile), :],
            send_sem=v_send.at[g], recv_sem=v_recv.at[tile],
            device_id=column(g), device_id_type=MESH)

    def q_copy(g, tile, half):
        return pltpu.make_async_remote_copy(
            src_ref=q_ref.at[:, cols(g * 2 + half, HALF)],
            dst_ref=qb.at[half, tile],
            send_sem=q_send.at[half, g], recv_sem=q_recv.at[half, tile],
            device_id=column(g), device_id_type=MESH)

    def x1_copy(j):
        return pltpu.make_async_remote_copy(
            src_ref=kvb.at[:, rows(16 + j), :],
            dst_ref=kvb.at[:, rows(8 + j), :],
            send_sem=x1_send.at[j], recv_sem=x1_recv.at[j],
            device_id=along(ahead), device_id_type=MESH)

    def x2_copy(j):
        return pltpu.make_async_remote_copy(
            src_ref=kvb.at[:, rows(8 + j), :],
            dst_ref=kvb.at[:, rows(j), :],
            send_sem=x2_send.at[j], recv_sem=x2_recv.at[j],
            device_id=along(ahead), device_id_type=MESH)

    def goes_round(j):
        return (lax.rem(j, 2) == 1) | (j == 6)

    def relay_copy(j):
        return pltpu.make_async_remote_copy(
            src_ref=kvb.at[:, rows(16 + j), :],
            dst_ref=relay.at[j],
            send_sem=relay_send.at[j], recv_sem=relay_recv.at[j],
            device_id=along(relay_to), device_id_type=MESH)

    def final_copy(j):
        return pltpu.make_async_remote_copy(
            src_ref=relay.at[j],
            dst_ref=kvb.at[:, rows(j), :],
            send_sem=final_send.at[j], recv_sem=x2_recv.at[j],
            device_id=along(final_to), device_id_type=MESH)

    def o_copy(g, tile, half):
        target = {"head": lax.rem(tile, 4), "doc": c * 2 + lax.div(tile, 4)}
        return pltpu.make_async_remote_copy(
            src_ref=ob.at[half, tile],
            dst_ref=o_ref.at[:, cols(g * 2 + half, HALF)],
            send_sem=o_send.at[half, tile], recv_sem=o_recv.at[half, g],
            device_id=target, device_id_type=MESH)

    sends_one = c < CHIPS - 1
    sends_two = (c < CHIPS - 1) & (c > 0)
    starts_relay = c < CHIPS - 2
    is_relay = y * 4 + lax.rem(x + 3, 4) >= 2
    takes_one = c > 0
    takes_two = c > 1

    def turn(tile):
        kt[:HEAD_SIZE, rows(tile)] = kvb[0, rows(tile), :].T

    def pass_own(j):
        k_copy(my_head, j).wait_recv()
        v_copy(my_head, j).wait_recv()

        @pl.when(sends_one)
        def _():
            x1_copy(j).start()

        @pl.when(starts_relay & goes_round(j))
        def _():
            relay_copy(j).start()

    def pass_round(j):
        @pl.when(is_relay)
        def _():
            relay_copy(j).wait_recv()
            final_copy(j).start()

    def pass_on(j):
        @pl.when(takes_one)
        def _():
            x1_copy(j).wait_recv()

        @pl.when(sends_two & jnp.logical_not(goes_round(j)))
        def _():
            x2_copy(j).start()

    arrivals = [my_tile]
    for (dz0, core0), (dz1, core1) in zip(FROM_FIRST, FROM_SECOND):
        first_core = core == 0
        zz = lax.rem(z + jnp.where(first_core, dz0, dz1), 4)
        arrivals.append(jnp.where(first_core, core0, core1) * 4 + zz)

    def send_kv(at):
        g, _ = place(*at)
        k_copy(g, my_tile).start()
        v_copy(g, my_tile).start()

    def send_q():
        for half in range(2):
            for at in NEAREST[1:]:
                g, _ = place(*at)
                q_copy(g, my_tile, half).start()

    send_kv(NEAREST[1])

    @pl.when(core == 1)
    def _():
        for at in NEAREST[2:]:
            send_kv(at)

    for half in range(2):
        pltpu.make_async_copy(
            q_ref.at[:, cols(my_head * 2 + half, HALF)], qb.at[half, my_tile], q_recv.at[half, my_tile]
        ).start()
    pass_own(my_tile)

    @pl.when(core == 1)
    def _():
        send_q()

    for r, j in enumerate(arrivals[1:]):
        pass_own(j)
        if r == HELD:
            @pl.when(core == 0)
            def _():
                for at in NEAREST[2:]:
                    send_kv(at)
                send_q()

    for r, j in enumerate(arrivals):
        turn(REACH + j)
        if r < 3:
            pass_round(RELAYED[r])
    for r, j in enumerate(arrivals):
        pass_on(j)
        turn(CHIP_TILES + j)
        if r in (2, 4):
            pass_round(RELAYED[3 + r // 4])

    ones = jnp.ones(((REACH + 1) * TILE, 128), jnp.bfloat16)
    span = (REACH + 1) * TILE
    causal = lax.broadcasted_iota(jnp.int32, (TILE, TILE), 1) <= lax.broadcasted_iota(
        jnp.int32, (TILE, TILE), 0)

    def scores(half, j, h):
        queries = qb[half, j, :, h * HEAD_SIZE:(h + 1) * HEAD_SIZE]
        left = jnp.concatenate([queries, feat_q[rows(j), :]], axis=1)
        s = jnp.dot(left, kt[:, rows(j, REACH + 1)], preferred_element_type=jnp.float32)
        return jnp.concatenate(
            [s[:, :span - TILE], jnp.where(causal, s[:, span - TILE:], HIDDEN)], axis=1)

    def weigh(half, j, h, s):
        highest = s[:, :128]
        for g in range(128, span, 128):
            highest = jnp.maximum(highest, s[:, g:g + 128])
        highest = jnp.max(highest, axis=1, keepdims=True)
        weights = jnp.exp2((s - highest) * SCALE).astype(jnp.bfloat16)
        values = jnp.concatenate([kvb[1, rows(j, REACH + 1), :], ones], axis=1)
        summed = jnp.dot(weights, values, preferred_element_type=jnp.float32)
        out = summed[:, :HEAD_SIZE] / summed[:, HEAD_SIZE:]
        ob[half, j, :, h * HEAD_SIZE:(h + 1) * HEAD_SIZE] = out.astype(jnp.bfloat16)

    def attend(half, tiles):
        units = [(j, h) for j in tiles for h in range(2)]
        scored = [scores(half, j, h) for j, h in units]
        for (j, h), s in zip(units, scored):
            weigh(half, j, h, s)
        for j in tiles:
            @pl.when(j != my_tile)
            def _():
                o_copy(my_head, j, half).start()

            @pl.when(j == my_tile)
            def _():
                pltpu.make_async_copy(
                    ob.at[half, j], o_ref.at[:, cols(my_head * 2 + half, HALF)],
                    o_recv.at[half, my_head]
                ).start()

    def first_half(t, _):
        tiles = (CHIP_TILES - 1 - 2 * t, CHIP_TILES - 2 - 2 * t)
        for j in tiles:
            q_copy(my_head, j, 0).wait_recv()

            @pl.when(takes_two)
            def _():
                x2_copy(j).wait_recv()

            turn(j)
        attend(0, tiles)
        return 0

    def second_half(t, _):
        outer, last = t == 0, t == 3
        tiles = (
            place(jnp.where(outer, 2, jnp.where(last, 0, 3)), jnp.where(t == 2, 0, 1))[1],
            place(jnp.where(outer, 2, jnp.where(last, 0, 1)), jnp.where(t == 1, 1, 0))[1],
        )
        for j in tiles:
            q_copy(my_head, j, 1).wait_recv()
        attend(1, tiles)
        return 0

    lax.fori_loop(0, CHIP_TILES // 2, first_half, 0)
    lax.fori_loop(0, CHIP_TILES // 2, second_half, 0)
    for r, at in enumerate(NEAREST):
        g, j = place(*at)

        @pl.when(sends_one)
        def _():
            x1_copy(j).wait_send()

        @pl.when(starts_relay & goes_round(j))
        def _():
            relay_copy(j).wait_send()

        @pl.when(sends_two & jnp.logical_not(goes_round(j)))
        def _():
            x2_copy(j).wait_send()

        if r < len(RELAYED):
            @pl.when(is_relay)
            def _():
                final_copy(RELAYED[r]).wait_send()

        if r > 0:
            k_copy(g, my_tile).wait_send()
            v_copy(g, my_tile).wait_send()
        for half in range(2):
            if r > 0:
                q_copy(g, my_tile, half).wait_send()
                o_copy(my_head, j, half).wait_send()
            o_copy(g, my_tile, half).wait_recv()


def on_device(packed_query_rows, packed_key_rows, packed_value_rows, doc_lengths):
    anywhere = pl.BlockSpec(memory_space=pl.ANY)
    bf16, f32 = jnp.bfloat16, jnp.float32
    dma = pltpu.SemaphoreType.DMA((CHIP_TILES,))
    halves = pltpu.SemaphoreType.DMA((2, CHIP_TILES))
    window = WINDOW_TILES * TILE
    return pl.pallas_call(
        kernel,
        out_shape=jax.ShapeDtypeStruct(packed_query_rows.shape, bf16),
        in_specs=[pl.BlockSpec(memory_space=pltpu.SMEM), anywhere, anywhere, anywhere],
        out_specs=anywhere,
        scratch_shapes=[
            pltpu.VMEM((2, CHIP_TILES, TILE, HALF), bf16),
            pltpu.VMEM((2, window, HEAD_SIZE), bf16),
            pltpu.VMEM((2 * HEAD_SIZE, window), bf16),
            pltpu.VMEM((CHIP_TILES, 2, TILE, HEAD_SIZE), bf16),
            pltpu.VMEM((CHIP_TILES * TILE, 128), bf16),
            pltpu.VMEM((2, CHIP_TILES, TILE, HALF), bf16),
        ] + [halves] * 2 + [dma] * 11 + [halves] * 2,
        compiler_params=pltpu.CompilerParams(
            collective_id=0, has_side_effects=True, vmem_limit_bytes=60 * 1024 * 1024),
        name="attention",
    )(doc_lengths, packed_query_rows, packed_key_rows, packed_value_rows)


def solution(mesh):
    token = P(("doc", "head"), None)
    return jax.shard_map(
        on_device, mesh=mesh, in_specs=(token, token, token, P()), out_specs=token, check_vma=False)
```

```python
import functools
import math

import jax
import jax.numpy as jnp
from jax import lax
from jax.experimental import pallas as pl
from jax.experimental.pallas import tpu as pltpu
from jax.sharding import PartitionSpec as P

HEAD_SIZE = 128
TILE = 128
CHIP_TILES = 8
WINDOW_TILES = 24
REACH = 16
DOCS = 64
SCALE = math.log2(math.e) / math.sqrt(HEAD_SIZE)
HIDDEN = -1e30
MESH = pl.DeviceIdType.MESH
RELAYED = (7, 6, 5, 4, 2)
HALF = 2 * HEAD_SIZE
CHIPS = 16
FROM_FIRST = ((0, 1), (1, 1), (3, 1), (2, 1), (1, 0), (3, 0), (2, 0))
FROM_SECOND = ((1, 1), (3, 1), (2, 1), (0, 0), (1, 0), (3, 0), (2, 0))
AFTER_OWN = {4: (7,), 5: (6,), 6: (5,)}
AFTER_CHAINED = {0: (4,), 2: (2,)}
HELD = 0
NEAREST = ((0, 0), (0, 1), (1, 0), (3, 0), (1, 1), (3, 1), (2, 0), (2, 1))


def kernel(
    lens_ref, q_ref, k_ref, v_ref, o_ref,
    qb, kvb, kt, relay, feat_q, ob,
    q_send, q_recv, k_send, k_recv, v_send, v_recv,
    x1_send, x1_recv, x2_send, x2_recv, relay_send, relay_recv, final_send, o_send, o_recv,
):
    z = lax.axis_index("head")
    d = lax.axis_index("doc")
    core = lax.rem(d, 2)
    c = lax.div(d, 2)
    x = lax.rem(c, 4)
    y = lax.div(c, 4)
    my_tile = core * 4 + z
    my_head = z * 2 + core

    def chip(yy, xx):
        return (lax.rem(yy + 4, 4) * 4 + lax.rem(xx + 4, 4)) * 2 + core

    ahead = lax.rem(d + 2, 32)
    behind = lax.rem(d + 30, 32)
    relay_to = chip(y + jnp.where(x >= 2, 1, 0), x - 1)
    relay_source = chip(y - jnp.where((x == 1) | (x == 2), 1, 0), x + 1)
    final_to = chip(y, x - 1)
    final_from = chip(y, x + 1)

    def column(g):
        return {"head": lax.div(g, 2), "doc": c * 2 + lax.rem(g, 2)}

    def along(dd):
        return {"head": z, "doc": dd}

    def rows(tile, count=1):
        return pl.ds(pl.multiple_of(tile * TILE, TILE), TILE * count)

    def cols(g, width):
        return pl.ds(pl.multiple_of(g * width, width), width)

    pltpu.make_async_copy(
        k_ref.at[:, cols(my_head, HEAD_SIZE)], kvb.at[0, rows(REACH + my_tile), :], k_recv.at[my_tile]
    ).start()
    pltpu.make_async_copy(
        v_ref.at[:, cols(my_head, HEAD_SIZE)], kvb.at[1, rows(REACH + my_tile), :], v_recv.at[my_tile]
    ).start()
    barrier = pltpu.get_barrier_semaphore()

    def greet(i, _):
        g = lax.rem(my_head + i, 8)
        pl.semaphore_signal(barrier, inc=1, device_id=column(g), device_id_type=MESH)
        return 0

    lax.fori_loop(1, 8, greet, 0)
    for other in (behind, relay_source, final_from):
        pl.semaphore_signal(barrier, inc=1, device_id=along(other), device_id_type=MESH)
    pl.semaphore_wait(barrier, 10)


    def place(dz, dcore):
        zz, cc = lax.rem(z + dz, 4), lax.rem(core + dcore, 2)
        return zz * 2 + cc, cc * 4 + zz

    def k_copy(g, tile):
        return pltpu.make_async_remote_copy(
            src_ref=k_ref.at[:, cols(g, HEAD_SIZE)],
            dst_ref=kvb.at[0, rows(REACH + tile), :],
            send_sem=k_send.at[g], recv_sem=k_recv.at[tile],
            device_id=column(g), device_id_type=MESH)

    def v_copy(g, tile):
        return pltpu.make_async_remote_copy(
            src_ref=v_ref.at[:, cols(g, HEAD_SIZE)],
            dst_ref=kvb.at[1, rows(REACH + tile), :],
            send_sem=v_send.at[g], recv_sem=v_recv.at[tile],
            device_id=column(g), device_id_type=MESH)

    def q_copy(g, tile, half):
        return pltpu.make_async_remote_copy(
            src_ref=q_ref.at[:, cols(g * 2 + half, HALF)],
            dst_ref=qb.at[half, tile],
            send_sem=q_send.at[half, g], recv_sem=q_recv.at[half, tile],
            device_id=column(g), device_id_type=MESH)

    def x1_copy(j):
        return pltpu.make_async_remote_copy(
            src_ref=kvb.at[:, rows(16 + j), :],
            dst_ref=kvb.at[:, rows(8 + j), :],
            send_sem=x1_send.at[j], recv_sem=x1_recv.at[j],
            device_id=along(ahead), device_id_type=MESH)

    def x2_copy(j):
        return pltpu.make_async_remote_copy(
            src_ref=kvb.at[:, rows(8 + j), :],
            dst_ref=kvb.at[:, rows(j), :],
            send_sem=x2_send.at[j], recv_sem=x2_recv.at[j],
            device_id=along(ahead), device_id_type=MESH)

    def goes_round(j):
        return functools.reduce(jnp.logical_or, [j == tile for tile in RELAYED])

    def relay_copy(j):
        return pltpu.make_async_remote_copy(
            src_ref=kvb.at[:, rows(16 + j), :],
            dst_ref=relay.at[j],
            send_sem=relay_send.at[j], recv_sem=relay_recv.at[j],
            device_id=along(relay_to), device_id_type=MESH)

    def final_copy(j):
        return pltpu.make_async_remote_copy(
            src_ref=relay.at[j],
            dst_ref=kvb.at[:, rows(j), :],
            send_sem=final_send.at[j], recv_sem=x2_recv.at[j],
            device_id=along(final_to), device_id_type=MESH)

    def o_copy(g, tile, half):
        target = {"head": lax.rem(tile, 4), "doc": c * 2 + lax.div(tile, 4)}
        return pltpu.make_async_remote_copy(
            src_ref=ob.at[half, tile],
            dst_ref=o_ref.at[:, cols(g * 2 + half, HALF)],
            send_sem=o_send.at[half, tile], recv_sem=o_recv.at[half, g],
            device_id=target, device_id_type=MESH)

    sends_one = c < CHIPS - 1
    sends_two = (c < CHIPS - 1) & (c > 0)
    starts_relay = c < CHIPS - 2
    is_relay = y * 4 + lax.rem(x + 3, 4) >= 2
    takes_one = c > 0
    takes_two = c > 1

    def turn(tile):
        kt[:HEAD_SIZE, rows(tile)] = kvb[0, rows(tile), :].T

    def pass_own(j):
        k_copy(my_head, j).wait_recv()
        v_copy(my_head, j).wait_recv()

        @pl.when(sends_one)
        def _():
            x1_copy(j).start()

        @pl.when(starts_relay & goes_round(j))
        def _():
            relay_copy(j).start()

    def pass_round(j):
        @pl.when(is_relay)
        def _():
            relay_copy(j).wait_recv()
            final_copy(j).start()

    def pass_on(j):
        @pl.when(takes_one)
        def _():
            x1_copy(j).wait_recv()

        @pl.when(sends_two & jnp.logical_not(goes_round(j)))
        def _():
            x2_copy(j).start()

    arrivals = [my_tile]
    for (dz0, core0), (dz1, core1) in zip(FROM_FIRST, FROM_SECOND):
        first_core = core == 0
        zz = lax.rem(z + jnp.where(first_core, dz0, dz1), 4)
        arrivals.append(jnp.where(first_core, core0, core1) * 4 + zz)

    def send_kv(at):
        g, _ = place(*at)
        k_copy(g, my_tile).start()
        v_copy(g, my_tile).start()

    def send_q():
        for half in range(2):
            for dz, dcore in NEAREST[1:]:
                g, _ = place(lax.rem(jnp.where(core == 0, dz, 4 - dz), 4), dcore)
                q_copy(g, my_tile, half).start()

    pass_own(my_tile)
    send_kv(NEAREST[1])

    @pl.when(core == 1)
    def _():
        for at in NEAREST[2:]:
            send_kv(at)

    for half in range(2):
        pltpu.make_async_copy(
            q_ref.at[:, cols(my_head * 2 + half, HALF)], qb.at[half, my_tile], q_recv.at[half, my_tile]
        ).start()

    @pl.when(core == 1)
    def _():
        send_q()

    @pl.when(c == 0)
    def _():
        kvb[:, 0:REACH * TILE, :] = jnp.zeros((2, REACH * TILE, HEAD_SIZE), jnp.bfloat16)

    @pl.when(c == 1)
    def _():
        kvb[:, 0:CHIP_TILES * TILE, :] = jnp.zeros((2, CHIP_TILES * TILE, HEAD_SIZE), jnp.bfloat16)

    lane = lax.broadcasted_iota(jnp.int32, (1, 128), 1)

    def add_document(i, bounds):
        first, end = bounds
        length = lens_ref[i]
        return first + jnp.where(lane > i, length, 0), end + jnp.where(lane >= i, length, 0)

    zero = jnp.zeros((1, 128), jnp.int32)
    first, end = lax.fori_loop(0, DOCS, add_document, (zero, zero))
    first = jnp.where(lane == DOCS, -(1 << 30), first)
    end = jnp.where(lane == DOCS, 0, end)
    line = lax.broadcasted_iota(jnp.int32, (TILE, 128), 0)

    def member(tile):
        token = line + (c * CHIP_TILES - REACH + tile) * TILE
        return (token >= first) & (token < end)

    def key_features(tile, _):
        kt[HEAD_SIZE:, rows(tile)] = jnp.where(member(tile), 1.0, 0.0).astype(jnp.bfloat16).T
        return 0

    def query_features(tile, _):
        feat_q[rows(tile), :] = jnp.where(member(tile + REACH), 0.0, HIDDEN).astype(jnp.bfloat16)
        return 0

    def mark_documents():
        lax.fori_loop(0, WINDOW_TILES, key_features, 0)
        lax.fori_loop(0, CHIP_TILES, query_features, 0)

    for r, j in enumerate(arrivals[1:]):
        pass_own(j)
        if r == HELD:
            @pl.when(core == 0)
            def _():
                for at in NEAREST[2:]:
                    send_kv(at)
                send_q()
        if r == 0:
            mark_documents()
        for tile in AFTER_OWN.get(r, ()):
            pass_round(tile)

    for r, j in enumerate(arrivals):
        turn(REACH + j)
    for r, j in enumerate(arrivals):
        pass_on(j)
        turn(CHIP_TILES + j)
        for tile in AFTER_CHAINED.get(r, ()):
            pass_round(tile)

    ones = jnp.ones(((REACH + 1) * TILE, 128), jnp.bfloat16)
    span = (REACH + 1) * TILE
    causal = lax.broadcasted_iota(jnp.int32, (TILE, TILE), 1) <= lax.broadcasted_iota(
        jnp.int32, (TILE, TILE), 0)

    def scores(half, j, h):
        queries = qb[half, j, :, h * HEAD_SIZE:(h + 1) * HEAD_SIZE]
        left = jnp.concatenate([queries, feat_q[rows(j), :]], axis=1)
        s = jnp.dot(left, kt[:, rows(j, REACH + 1)], preferred_element_type=jnp.float32)
        return jnp.concatenate(
            [s[:, :span - TILE], jnp.where(causal, s[:, span - TILE:], HIDDEN)], axis=1)

    def weigh(half, j, h, s):
        highest = s[:, :128]
        for g in range(128, span, 128):
            highest = jnp.maximum(highest, s[:, g:g + 128])
        highest = jnp.max(highest, axis=1, keepdims=True)
        weights = jnp.exp2((s - highest) * SCALE).astype(jnp.bfloat16)
        values = jnp.concatenate([kvb[1, rows(j, REACH + 1), :], ones], axis=1)
        summed = jnp.dot(weights, values, preferred_element_type=jnp.float32)
        out = summed[:, :HEAD_SIZE] / summed[:, HEAD_SIZE:]
        ob[half, j, :, h * HEAD_SIZE:(h + 1) * HEAD_SIZE] = out.astype(jnp.bfloat16)

    def attend(half, tiles):
        units = [(j, h) for j in tiles for h in range(2)]
        scored = [scores(half, j, h) for j, h in units]
        for (j, h), s in zip(units, scored):
            weigh(half, j, h, s)
        for j in tiles:
            @pl.when(j != my_tile)
            def _():
                o_copy(my_head, j, half).start()

            @pl.when(j == my_tile)
            def _():
                pltpu.make_async_copy(
                    ob.at[half, j], o_ref.at[:, cols(my_head * 2 + half, HALF)],
                    o_recv.at[half, my_head]
                ).start()

    def first_half(t, _):
        tiles = (CHIP_TILES - 1 - 2 * t, CHIP_TILES - 2 - 2 * t)
        for j in tiles:
            q_copy(my_head, j, 0).wait_recv()

            @pl.when(takes_two)
            def _():
                x2_copy(j).wait_recv()

            turn(j)
        attend(0, tiles)
        return 0

    def second_half(t, _):
        outer, last = t == 0, t == 3
        tiles = (
            place(jnp.where(outer, 2, jnp.where(last, 0, 3)), jnp.where(t == 2, 0, 1))[1],
            place(jnp.where(outer, 2, jnp.where(last, 0, 1)), jnp.where(t == 1, 1, 0))[1],
        )
        for j in tiles:
            q_copy(my_head, j, 1).wait_recv()
        attend(1, tiles)
        return 0

    lax.fori_loop(0, CHIP_TILES // 2, first_half, 0)
    lax.fori_loop(0, CHIP_TILES // 2, second_half, 0)
    for r, at in enumerate(NEAREST):
        g, j = place(*at)

        @pl.when(sends_one)
        def _():
            x1_copy(j).wait_send()

        @pl.when(starts_relay & goes_round(j))
        def _():
            relay_copy(j).wait_send()

        @pl.when(sends_two & jnp.logical_not(goes_round(j)))
        def _():
            x2_copy(j).wait_send()

        if r < len(RELAYED):
            @pl.when(is_relay)
            def _():
                final_copy(RELAYED[r]).wait_send()

        if r > 0:
            k_copy(g, my_tile).wait_send()
            v_copy(g, my_tile).wait_send()
        for half in range(2):
            if r > 0:
                q_copy(g, my_tile, half).wait_send()
                o_copy(my_head, j, half).wait_send()
            o_copy(g, my_tile, half).wait_recv()


def on_device(packed_query_rows, packed_key_rows, packed_value_rows, doc_lengths):
    anywhere = pl.BlockSpec(memory_space=pl.ANY)
    bf16, f32 = jnp.bfloat16, jnp.float32
    dma = pltpu.SemaphoreType.DMA((CHIP_TILES,))
    halves = pltpu.SemaphoreType.DMA((2, CHIP_TILES))
    window = WINDOW_TILES * TILE
    return pl.pallas_call(
        kernel,
        out_shape=jax.ShapeDtypeStruct(packed_query_rows.shape, bf16),
        in_specs=[pl.BlockSpec(memory_space=pltpu.SMEM), anywhere, anywhere, anywhere],
        out_specs=anywhere,
        scratch_shapes=[
            pltpu.VMEM((2, CHIP_TILES, TILE, HALF), bf16),
            pltpu.VMEM((2, window, HEAD_SIZE), bf16),
            pltpu.VMEM((2 * HEAD_SIZE, window), bf16),
            pltpu.VMEM((CHIP_TILES, 2, TILE, HEAD_SIZE), bf16),
            pltpu.VMEM((CHIP_TILES * TILE, 128), bf16),
            pltpu.VMEM((2, CHIP_TILES, TILE, HALF), bf16),
        ] + [halves] * 2 + [dma] * 11 + [halves] * 2,
        compiler_params=pltpu.CompilerParams(
            collective_id=0, has_side_effects=True, vmem_limit_bytes=60 * 1024 * 1024),
        name="attention",
    )(doc_lengths, packed_query_rows, packed_key_rows, packed_value_rows)


def solution(mesh):
    token = P(("doc", "head"), None)
    return jax.shard_map(
        on_device, mesh=mesh, in_specs=(token, token, token, P()), out_specs=token, check_vma=False)
```
